32 devices in a mesh: head: 4 (over y, x), tile: 8 (over z, core).
Axes of the slice: x: 2, y: 2, z: 4, core: 2. Of those that a mesh axis runs over, the one named last changes fastest.
Arguments:
- hidden: bfloat16 [8, 384, 1536], P(None, ('head', 'tile')), may hold values from -6 to 6
- latent: float32 [8, 384, 64], P(None, ('head', 'tile')), may hold values from -6 to 6
- cell_map: int32 [8, 384], P(None, ('head', 'tile')), may hold values from 0 to 383, each once within a row
- text_lengths: int32 [8], P('tile'), may hold values from 64 to 512, as said below
- block_modulation: float32 [8, 3, 1536], replicated, may hold values from -3 to 3
- head_modulation: float32 [8, 2, 1536], replicated, may hold values from -3 to 3
- step_sizes: float32 [8], replicated, may hold values from -0.5 to -0.1
- w_qkv: bfloat16 [1536, 4608], replicated, may hold values from -0.15625 to 0.15625
- self_q_gain: float32 [1536], replicated, may hold values from 0.5 to 2
- self_k_gain: float32 [1536], replicated, may hold values from 0.5 to 2
- w_out: bfloat16 [1536, 1536], replicated, may hold values from -0.15625 to 0.15625
- cross_gain: float32 [1536], replicated, may hold values from 0.1 to 1.9
- cross_wq: bfloat16 [1536, 1536], P(None, 'head'), may hold values from -0.15625 to 0.15625
- cross_q_gain: float32 [1536], P('head'), may hold values from 0.5 to 2
- text_keys: bfloat16 [8, 512, 1536], P('tile', None, 'head'), may hold values from -2.5 to 2.5
- text_values: bfloat16 [8, 512, 1536], P('tile', None, 'head'), may hold values from -4 to 4
- cross_wo: bfloat16 [1536, 1536], P('head'), may hold values from -0.15625 to 0.15625
- head_w: bfloat16 [1536, 64], replicated, may hold values from -0.15625 to 0.15625
Outputs:
- hidden_next: bfloat16 [8, 384, 1536], P(None, ('head', 'tile'))
- latent_next: float32 [8, 384, 64], P(None, ('head', 'tile'))
The draws below stay inside these ranges and needn't reach their ends.
Inputs may be any that keep to these rules, and one draw needn't show every extreme that they name: Each row cell_map[v] names every cell of video v once. Text positions from text_lengths[v] on are padding of video v.
All inputs are finite; a program needn't handle non-finite values.
Results may differ from the reference program's by a relative error of at most 0.007.
Values may be sent and summed in bfloat16 or wider, within the bound.
A program may use at most 128 MiB of HBM per device.

```python
import math
import jax
import jax.numpy as jnp
from jax import lax

D = 1536
HEADS = 12
HEAD_DIM = 128
TEXT = 512
OUT_CH = 64
GRID_H = 24
GRID_W = 8
VIDEO_TOK = 384
VIDEOS = 8


def draw_text_lengths(key, part):
    lengths_drawn = jax.random.randint(jax.random.fold_in(key, 11), (VIDEOS,), TEXT // 8, TEXT + 1)
    chosen = jax.random.randint(jax.random.fold_in(key, 12), (), 0, VIDEOS)
    places = jnp.arange(VIDEOS)
    lengths_drawn = jnp.where(places == chosen, TEXT, lengths_drawn)
    lengths_drawn = jnp.where(places == (chosen + 1) % VIDEOS, TEXT // 8, lengths_drawn)
    return lengths_drawn.astype(jnp.int32)


def block_levels(stream_key, dims, cuts, smallest, largest):
    level = 1.0
    for axis_at, parts in cuts:
        steps = jax.random.uniform(jax.random.fold_in(jax.random.fold_in(stream_key, 6), axis_at), (parts,), jnp.float32, smallest / len(cuts), largest / len(cuts))
        level = level * jnp.repeat(jnp.exp(steps), dims[axis_at] // parts).reshape((-1,) + (1,) * (len(dims) - 1 - axis_at))
    return level


def noise(stream_key, extent, deviation, most, cuts=(), kind=jnp.bfloat16):
    result = deviation * jax.random.normal(stream_key, extent, jnp.float32)
    if cuts:
        result = result * block_levels(stream_key, extent, cuts, -0.22, 0.18)
    return jnp.clip(result, -most, most).astype(kind)


def setup_inputs(seed: int = 0) -> dict:
    key_list = jax.random.split(jax.random.key(seed), 19)
    return {
        "hidden": noise(key_list[0], (VIDEOS, VIDEO_TOK, D), 1.0, 6.0, ((1, 32),)),
        "latent": noise(key_list[1], (VIDEOS, VIDEO_TOK, OUT_CH), 1.0, 6.0, ((1, 32),), jnp.float32),
        "cell_map": jax.vmap(lambda own: jax.random.permutation(own, VIDEO_TOK))(jax.random.split(key_list[2], VIDEOS)).reshape((VIDEOS, VIDEO_TOK)).astype(jnp.int32),
        "text_lengths": draw_text_lengths(jax.random.fold_in(key_list[18], 71), 0),
        "block_modulation": noise(key_list[4], (VIDEOS, 3, D), 0.7, 3.0, (), jnp.float32),
        "head_modulation": noise(key_list[5], (VIDEOS, 2, D), 0.7, 3.0, (), jnp.float32),
        "step_sizes": jnp.clip(jax.random.uniform(key_list[6], (VIDEOS,), jnp.float32, -0.5, -0.1), -0.5, -0.1),
        "w_qkv": noise(key_list[7], (D, 3 * D), D ** -0.5, 0.15625),
        "self_q_gain": jnp.clip(jax.random.uniform(key_list[8], (D,), jnp.float32, 0.5, 2.0), 0.5, 2.0),
        "self_k_gain": jnp.clip(jax.random.uniform(key_list[9], (D,), jnp.float32, 0.5, 2.0), 0.5, 2.0),
        "w_out": noise(key_list[10], (D, D), D ** -0.5, 0.15625),
        "cross_gain": jnp.clip(1.0 + 0.18 * jax.random.normal(key_list[11], (D,), jnp.float32), 0.1, 1.9),
        "cross_wq": noise(key_list[12], (D, D), D ** -0.5, 0.15625, ((1, 4),)),
        "cross_q_gain": jnp.clip(0.5 + 1.5 * jax.random.uniform(key_list[13], (D,), jnp.float32) ** block_levels(key_list[13], (D,), ((0, 4),), -0.2, 0.2), 0.5, 2.0),
        "text_keys": noise(key_list[14], (VIDEOS, TEXT, D), 1.0, 2.5, ((0, 8), (2, 4))),
        "text_values": noise(key_list[15], (VIDEOS, TEXT, D), 1.0, 4.0, ((0, 8), (2, 4))),
        "cross_wo": noise(key_list[16], (D, D), D ** -0.5, 0.15625, ((0, 4),)),
        "head_w": noise(key_list[17], (D, OUT_CH), D ** -0.5, 0.15625),
    }


EPSILON = 1e-06

def rounded(inputs):
    return lax.optimization_barrier(inputs.astype(jnp.bfloat16))

def layer_norm(inputs):
    average = lax.optimization_barrier(jnp.mean(inputs, axis=-1, keepdims=True))
    centred = inputs - average
    variance = lax.optimization_barrier(jnp.mean(centred * centred, axis=-1, keepdims=True))
    return centred * lax.rsqrt(variance + EPSILON)

def head_norm(inputs, gain_table):
    mean_square = lax.optimization_barrier(jnp.mean(inputs * inputs, axis=-1, keepdims=True))
    return inputs * lax.rsqrt(mean_square + EPSILON) * gain_table

def frequencies(pair_count):
    return jnp.power(10000.0, -jnp.arange(pair_count, dtype=jnp.float32) / pair_count)

def rope_angles(cell_ids):
    sixth_part = HEAD_DIM // 6
    time_pairs = HEAD_DIM // 2 - 2 * sixth_part
    plane_cells = GRID_H * GRID_W
    frame_index = (cell_ids // plane_cells).astype(jnp.float32)
    row_index = (cell_ids // GRID_W % GRID_H).astype(jnp.float32)
    column = (cell_ids % GRID_W).astype(jnp.float32)
    return jnp.concatenate([frame_index[..., None] * frequencies(time_pairs), row_index[..., None] * frequencies(sixth_part), column[..., None] * frequencies(sixth_part)], axis=-1)

def rotate(inputs, angles):
    half_dim = inputs.shape[-1] // 2
    cosine = jnp.cos(angles)[..., None, :]
    sine_part = jnp.sin(angles)[..., None, :]
    lower_half = inputs[..., :half_dim]
    upper_half = inputs[..., half_dim:]
    return jnp.concatenate([lower_half * cosine - upper_half * sine_part, lower_half * sine_part + upper_half * cosine], axis=-1)

def attention(queries, keys_all, values_all, live_mask):
    factor = 1.0 / math.sqrt(HEAD_DIM)
    scores = jnp.einsum('qhd,khd->hqk', queries.astype(jnp.float32), keys_all.astype(jnp.float32)) * factor
    weights = jnp.exp(scores) * live_mask
    totals = lax.optimization_barrier(jnp.sum(weights, axis=-1))
    mixture = jnp.einsum('hqk,khd->qhd', rounded(weights).astype(jnp.float32), values_all.astype(jnp.float32))
    return mixture / jnp.transpose(totals)[:, :, None]

def reference(hidden, latent, cell_map, text_lengths, block_modulation, head_modulation, step_sizes, w_qkv, self_q_gain, self_k_gain, w_out, cross_gain, cross_wq, cross_q_gain, text_keys, text_values, cross_wo, head_w):

    def one_video(video_items):
        hidden_item, latent_item, cells_item, length_item, block_item, head_item, step_item, keys_item, values_item = video_items
        stream = hidden_item.astype(jnp.float32)
        block_in = rounded(layer_norm(stream) * (1.0 + block_item[1]) + block_item[0])
        projected = jnp.dot(block_in, w_qkv, preferred_element_type=jnp.float32).reshape(VIDEO_TOK, 3, HEADS, HEAD_DIM)
        angles = rope_angles(cells_item)
        self_queries = rounded(rotate(head_norm(projected[:, 0], self_q_gain.reshape(HEADS, HEAD_DIM)), angles))
        self_keys = rounded(rotate(head_norm(projected[:, 1], self_k_gain.reshape(HEADS, HEAD_DIM)), angles))
        self_values = rounded(projected[:, 2])
        every_key = jnp.ones((VIDEO_TOK,), jnp.float32)
        attended = rounded(attention(self_queries, self_keys, self_values, every_key)).reshape(VIDEO_TOK, D)
        self_update = jnp.dot(attended, w_out, preferred_element_type=jnp.float32)
        after_self = stream + block_item[2] * self_update
        cross_in = rounded(layer_norm(after_self) * cross_gain)
        cross_queries = jnp.dot(cross_in, cross_wq, preferred_element_type=jnp.float32).reshape(VIDEO_TOK, HEADS, HEAD_DIM)
        cross_queries = rounded(head_norm(cross_queries, cross_q_gain.reshape(HEADS, HEAD_DIM)))
        live_mask = (jnp.arange(TEXT) < length_item).astype(jnp.float32)
        cross_mixed = rounded(attention(cross_queries, keys_item.reshape(TEXT, HEADS, HEAD_DIM), values_item.reshape(TEXT, HEADS, HEAD_DIM), live_mask)).reshape(VIDEO_TOK, D)
        cross_out = rounded(jnp.dot(cross_mixed, cross_wo, preferred_element_type=jnp.float32))
        after_cross = after_self + cross_out.astype(jnp.float32)
        hidden_next = after_cross.astype(jnp.bfloat16)
        head_in = rounded(layer_norm(after_cross) * (1.0 + head_item[1]) + head_item[0])
        velocity = jnp.dot(head_in, head_w, preferred_element_type=jnp.float32)
        latent_next = latent_item + step_item * velocity
        return (hidden_next, latent_next)
    return lax.map(one_video, (hidden, latent, cell_map, text_lengths, block_modulation, head_modulation, step_sizes, text_keys, text_values))
```

```python
import functools
import math

import jax
import jax.numpy as jnp
from jax import lax
from jax.experimental import pallas as pl
from jax.experimental.pallas import tpu as pltpu
from jax.sharding import PartitionSpec as P

HEADS = 12
HEAD_DIM = 128
GRID_H = 24
GRID_W = 8
PAD_ROWS = 16
EXTRA = 128
EPSILON = 1e-06
MESH = pl.DeviceIdType.MESH
F32 = jnp.float32
BF16 = jnp.bfloat16


def frequencies(pair_count):
    return jnp.power(10000.0, -jnp.arange(pair_count, dtype=jnp.float32) / pair_count)


def layer_norm(inputs):
    average = jnp.mean(inputs, axis=-1, keepdims=True)
    centred = inputs - average
    variance = jnp.mean(centred * centred, axis=-1, keepdims=True)
    return centred * lax.rsqrt(variance + EPSILON)


def head_norm(inputs, gain_row):
    mean_square = jnp.mean(inputs * inputs, axis=-1, keepdims=True)
    return inputs * lax.rsqrt(mean_square + EPSILON) * gain_row


def matmul(a, b):
    return jnp.dot(a, b, preferred_element_type=F32)


def matmul_t(a, b):
    return lax.dot_general(a, b, (((1,), (1,)), ((), ())), preferred_element_type=F32)


def kernel(
    tiles,
    per_video,
    ext_ref,
    length_ref,
    block_mod_ref,
    head_mod_ref,
    w_qkv_ref,
    q_gain_ref,
    k_gain_ref,
    w_out_ref,
    cross_gain_ref,
    wq_ref,
    cross_q_gain_ref,
    text_k_ref,
    text_v_ref,
    wo_ref,
    head_w_ref,
    freq_ref,
    hidden_out,
    velocity_out,
    rx,
    stream,
    gathered,
    q_buf,
    k_buf,
    v_buf,
    att_out,
    att_in,
    cross_in,
    part_out,
    part_in,
    own_part,
    next_rows,
    back_out,
    vel_rows,
    vel_out,
    back_in,
    vel_in,
    w_qkv,
    w_out,
    wq,
    wo,
    text_k,
    text_v,
    head_w,
    block_mod,
    head_mod,
    load_sem,
    s1_send,
    s1_recv,
    xy_send,
    xy_recv,
    back_send,
    back_recv,
):
    head = lax.axis_index("head")
    tile = lax.axis_index("tile")
    width = wq_ref.shape[0]
    group = wq_ref.shape[1]
    rows = tiles * per_video
    heads_here = group // HEAD_DIM
    factor = 1.0 / math.sqrt(HEAD_DIM)

    def partner(d):
        return lax.rem(head // 2 + d // 2, 2) * 2 + lax.rem(head % 2 + d % 2, 2)

    def tile_at(d):
        return lax.rem(tile + d + tiles, tiles)

    loads = []

    def load(src, dst):
        copy = pltpu.make_async_copy(src, dst, load_sem.at[len(loads)])
        copy.start()
        loads.append(copy)
        return copy

    load_own = load(ext_ref.at[tile], rx.at[tile])
    load_bm = load(block_mod_ref.at[tile], block_mod)
    load_hm = load(head_mod_ref.at[tile], head_mod)
    load_qkv = [
        load(
            w_qkv_ref.at[:, pl.ds(pl.multiple_of(i * width + head * group, 128), group)],
            w_qkv.at[i],
        )
        for i in range(3)
    ]

    barrier = pltpu.get_barrier_semaphore()
    for d in range(1, tiles):
        pl.semaphore_signal(barrier, inc=1, device_id=(head, tile_at(d)), device_id_type=MESH)
    for d in range(1, 4):
        pl.semaphore_signal(barrier, inc=1, device_id=(partner(d), tile), device_id_type=MESH)
    pl.semaphore_wait(barrier, tiles - 1 + 3)

    stage1 = []
    for d in range(1, tiles):
        to = tile_at(d)
        copy = pltpu.make_async_remote_copy(
            src_ref=ext_ref.at[to],
            dst_ref=rx.at[tile],
            send_sem=s1_send.at[d],
            recv_sem=s1_recv.at[d],
            device_id=(head, to),
            device_id_type=MESH,
        )
        copy.start()
        stage1.append(copy)

    load_out = load(w_out_ref, w_out)
    load_wq = load(wq_ref, wq)
    load_tk = load(text_k_ref.at[0], text_k)
    load_tv = load(text_v_ref.at[0], text_v)
    load_wo = load(wo_ref, wo)
    load_hw = load(head_w_ref, head_w)

    load_own.wait()
    for d in range(1, tiles):
        arrival = pltpu.make_async_remote_copy(
            src_ref=ext_ref.at[tile],
            dst_ref=rx.at[tile_at(-d)],
            send_sem=s1_send.at[d],
            recv_sem=s1_recv.at[d],
            device_id=(head, tile_at(-d)),
            device_id_type=MESH,
        )
        arrival.wait_recv()
    for t in range(tiles):
        stream[t * per_video : t * per_video + PAD_ROWS, :] = rx[t].astype(F32)
    load_bm.wait()
    hidden = stream[:rows, :width]
    block_in = layer_norm(hidden) * (1.0 + block_mod[1:2, :]) + block_mod[0:1, :]
    gathered[head, :, :width] = block_in.astype(BF16)
    gathered[head, :, width:] = stream[:rows, width:].astype(BF16)

    def exchange(step, src, dst, d):
        return pltpu.make_async_remote_copy(
            src_ref=src,
            dst_ref=dst,
            send_sem=xy_send.at[step, d],
            recv_sem=xy_recv.at[step, d],
            device_id=(partner(d), tile),
            device_id_type=MESH,
        )

    sends = []
    for d in range(1, 4):
        copy = exchange(0, gathered.at[head], gathered.at[head], d)
        copy.start()
        sends.append(copy)

    for copy in load_qkv:
        copy.wait()
    q_gain = q_gain_ref[head]
    k_gain = k_gain_ref[head]
    lane = lax.broadcasted_iota(jnp.int32, (1, HEAD_DIM), 1)
    sign = jnp.where(lane < HEAD_DIM // 2, -1.0, 1.0)
    for d in range(4):
        slot = partner(d)
        if d > 0:
            exchange(0, gathered.at[slot], gathered.at[slot], d).wait_recv()
        tokens = gathered[slot, :, :width]
        angles = gathered[slot, :, width:].astype(F32) * freq_ref[...]
        cosine = jnp.cos(angles)
        sine = jnp.sin(angles) * sign
        for i, (gain, buf) in enumerate(((q_gain, q_buf), (k_gain, k_buf))):
            raw = matmul(tokens, w_qkv[i])
            for g in range(heads_here):
                cols = slice(g * HEAD_DIM, (g + 1) * HEAD_DIM)
                u = head_norm(raw[:, cols], gain[g : g + 1, :])
                turned = u * cosine + pltpu.roll(u, HEAD_DIM // 2, 1) * sine
                buf[slot, :, cols] = turned.astype(BF16)
        v_buf[slot] = matmul(tokens, w_qkv[2]).astype(BF16)

    for d in (1, 2, 3, 0):
        slot = partner(d)
        for g in range(heads_here):
            cols = slice(g * HEAD_DIM, (g + 1) * HEAD_DIM)
            keys = k_buf[:, :, cols].reshape(4 * rows, HEAD_DIM)
            values = v_buf[:, :, cols].reshape(4 * rows, HEAD_DIM)
            weights = jnp.exp(matmul_t(q_buf[slot, :, cols], keys) * factor)
            total = jnp.sum(weights, axis=-1, keepdims=True)
            mixed = matmul(weights.astype(BF16), values) / total
            att_out[slot, :, cols] = mixed.astype(BF16)
        if d > 0:
            copy = exchange(1, att_out.at[slot], att_in.at[head], d)
            copy.start()
            sends.append(copy)

    load_out.wait()
    update = matmul(att_out[head], w_out[pl.ds(pl.multiple_of(head * group, 128), group), :])
    for d in range(1, 4):
        slot = partner(d)
        exchange(1, att_out.at[slot], att_in.at[slot], d).wait_recv()
        update += matmul(att_in[slot], w_out[pl.ds(pl.multiple_of(slot * group, 128), group), :])
    after_self = stream[:rows, :width] + block_mod[2:3, :] * update
    stream[:rows, :width] = after_self
    cross_in[head] = (layer_norm(after_self) * cross_gain_ref[...]).astype(BF16)
    for d in range(1, 4):
        copy = exchange(2, cross_in.at[head], cross_in.at[head], d)
        copy.start()
        sends.append(copy)

    for copy in (load_wq, load_tk, load_tv, load_wo):
        copy.wait()
    position = lax.broadcasted_iota(jnp.int32, (1, text_k.shape[0]), 1)
    live = jnp.where(position < length_ref[0], 1.0, 0.0)
    for d in range(4):
        slot = partner(d)
        if d > 0:
            exchange(2, cross_in.at[slot], cross_in.at[slot], d).wait_recv()
        raw = matmul(cross_in[slot], wq[...])
        mixes = []
        for g in range(heads_here):
            cols = slice(g * HEAD_DIM, (g + 1) * HEAD_DIM)
            query = head_norm(raw[:, cols], cross_q_gain_ref[g : g + 1, :]).astype(BF16)
            weights = jnp.exp(matmul_t(query, text_k[:, cols]) * factor) * live
            total = jnp.sum(weights, axis=-1, keepdims=True)
            mixes.append((matmul(weights.astype(BF16), text_v[:, cols]) / total).astype(BF16))
        product = matmul(jnp.concatenate(mixes, axis=-1), wo[...])
        if d == 0:
            own_part[...] = product
        else:
            part_out[d - 1] = product.astype(BF16)
            copy = exchange(3, part_out.at[d - 1], part_in.at[d - 1], d)
            copy.start()
            sends.append(copy)

    total = own_part[...]
    for d in range(1, 4):
        exchange(3, part_out.at[d - 1], part_in.at[d - 1], d).wait_recv()
        total += part_in[d - 1].astype(F32)
    after_cross = stream[:rows, :width] + total.astype(BF16).astype(F32)
    next_rows[:rows, :] = after_cross
    next_rows[rows:, :] = jnp.zeros((PAD_ROWS, width), F32)
    for t in range(tiles):
        back_out[t] = next_rows[t * per_video : t * per_video + PAD_ROWS, :].astype(BF16)

    def giving(kind, src, dst, d):
        return pltpu.make_async_remote_copy(
            src_ref=src,
            dst_ref=dst,
            send_sem=back_send.at[kind, d],
            recv_sem=back_recv.at[kind, d],
            device_id=(head, tile_at(d)),
            device_id_type=MESH,
        )

    for d in range(1, tiles):
        copy = giving(0, back_out.at[tile_at(d)], back_in.at[tile], d)
        copy.start()
        sends.append(copy)
    load_hm.wait()
    load_hw.wait()
    head_in = layer_norm(after_cross) * (1.0 + head_mod[1:2, :]) + head_mod[0:1, :]
    vel_rows[...] = jnp.zeros_like(vel_rows)
    vel_rows[:rows, : head_w.shape[1]] = matmul(head_in.astype(BF16), head_w[...])
    for t in range(tiles):
        vel_out[t] = vel_rows[t * per_video : t * per_video + PAD_ROWS, :]
    for d in range(1, tiles):
        copy = giving(1, vel_out.at[tile_at(d)], vel_in.at[tile], d)
        copy.start()
        sends.append(copy)
    hidden_out[tile] = back_out[tile]
    velocity_out[tile] = vel_out[tile]
    for d in range(1, tiles):
        source = tile_at(-d)
        giving(0, back_out.at[source], back_in.at[source], d).wait_recv()
        hidden_out[source] = back_in[source]
    for d in range(1, tiles):
        source = tile_at(-d)
        giving(1, vel_out.at[source], vel_in.at[source], d).wait_recv()
        velocity_out[source] = vel_in[source]
    for copy in stage1 + sends:
        copy.wait_send()


def local(
    hidden,
    latent,
    cell_map,
    text_lengths,
    block_modulation,
    head_modulation,
    step_sizes,
    w_qkv,
    self_q_gain,
    self_k_gain,
    w_out,
    cross_gain,
    cross_wq,
    cross_q_gain,
    text_keys,
    text_values,
    cross_wo,
    head_w,
):
    head_count = lax.axis_size("head")
    tiles = lax.axis_size("tile")
    videos, per_video, width = hidden.shape
    group = width // head_count
    heads_here = group // HEAD_DIM
    rows = tiles * per_video
    text = text_keys.shape[1]
    channels = head_w.shape[1]
    sixth = HEAD_DIM // 6
    time_pairs = HEAD_DIM // 2 - 2 * sixth

    lane = jnp.arange(EXTRA) % (HEAD_DIM // 2)
    cells = cell_map[..., None]
    places = jnp.where(
        lane < time_pairs,
        cells // (GRID_H * GRID_W),
        jnp.where(lane < time_pairs + sixth, cells // GRID_W % GRID_H, cells % GRID_W),
    ).astype(BF16)
    half = jnp.concatenate([frequencies(time_pairs), frequencies(sixth), frequencies(sixth)])
    freq = jnp.concatenate([half, half])[None, :]
    ext = jnp.pad(
        jnp.concatenate([hidden, places], axis=-1),
        ((0, 0), (0, PAD_ROWS - per_video), (0, 0)),
    )
    any_spec = pl.BlockSpec(memory_space=pl.ANY)
    vmem = pl.BlockSpec(memory_space=pltpu.VMEM)
    smem = pl.BlockSpec(memory_space=pltpu.SMEM)
    dma = pltpu.SemaphoreType.DMA
    hidden_pad, velocity = pl.pallas_call(
        functools.partial(kernel, tiles, per_video),
        out_shape=(
            jax.ShapeDtypeStruct((tiles, PAD_ROWS, width), BF16),
            jax.ShapeDtypeStruct((tiles, PAD_ROWS, 128), F32),
        ),
        in_specs=[
            any_spec,
            smem,
            any_spec,
            any_spec,
            any_spec,
            vmem,
            vmem,
            any_spec,
            vmem,
            any_spec,
            vmem,
            any_spec,
            any_spec,
            any_spec,
            any_spec,
            vmem,
        ],
        out_specs=(vmem, vmem),
        scratch_shapes=[
            pltpu.VMEM((tiles, PAD_ROWS, width + EXTRA), BF16),
            pltpu.VMEM((rows + PAD_ROWS, width + EXTRA), F32),
            pltpu.VMEM((head_count, rows, width + EXTRA), BF16),
            pltpu.VMEM((head_count, rows, group), BF16),
            pltpu.VMEM((head_count, rows, group), BF16),
            pltpu.VMEM((head_count, rows, group), BF16),
            pltpu.VMEM((head_count, rows, group), BF16),
            pltpu.VMEM((head_count, rows, group), BF16),
            pltpu.VMEM((head_count, rows, width), BF16),
            pltpu.VMEM((3, rows, width), BF16),
            pltpu.VMEM((3, rows, width), BF16),
            pltpu.VMEM((rows, width), F32),
            pltpu.VMEM((rows + PAD_ROWS, width), F32),
            pltpu.VMEM((tiles, PAD_ROWS, width), BF16),
            pltpu.VMEM((rows + PAD_ROWS, 128), F32),
            pltpu.VMEM((tiles, PAD_ROWS, 128), F32),
            pltpu.VMEM((tiles, PAD_ROWS, width), BF16),
            pltpu.VMEM((tiles, PAD_ROWS, 128), F32),
            pltpu.VMEM((3, width, group), BF16),
            pltpu.VMEM((width, width), BF16),
            pltpu.VMEM((width, group), BF16),
            pltpu.VMEM((group, width), BF16),
            pltpu.VMEM((text, group), BF16),
            pltpu.VMEM((text, group), BF16),
            pltpu.VMEM((width, channels), BF16),
            pltpu.VMEM((3, width), F32),
            pltpu.VMEM((2, width), F32),
            dma((12,)),
            dma((tiles,)),
            dma((tiles,)),
            dma((4, 4)),
            dma((4, 4)),
            dma((2, tiles)),
            dma((2, tiles)),
        ],
        compiler_params=pltpu.CompilerParams(
            collective_id=0, has_side_effects=True, vmem_limit_bytes=50 * 1024 * 1024
        ),
    )(
        ext,
        text_lengths,
        block_modulation,
        head_modulation,
        w_qkv,
        self_q_gain.reshape(head_count, heads_here, HEAD_DIM),
        self_k_gain.reshape(head_count, heads_here, HEAD_DIM),
        w_out,
        cross_gain.reshape(1, width),
        cross_wq,
        cross_q_gain.reshape(heads_here, HEAD_DIM),
        text_keys,
        text_values,
        cross_wo,
        head_w,
        freq,
    )
    hidden_next = hidden_pad[:, :per_video]
    latent_next = latent + step_sizes[:, None, None] * velocity[:, :per_video, :channels]
    return (hidden_next, latent_next)


def solution(mesh):
    return jax.shard_map(
        local,
        mesh=mesh,
        in_specs=(
            P(None, ("head", "tile"), None),
            P(None, ("head", "tile"), None),
            P(None, ("head", "tile")),
            P("tile"),
            P(),
            P(),
            P(),
            P(),
            P(),
            P(),
            P(),
            P(),
            P(None, "head"),
            P("head"),
            P("tile", None, "head"),
            P("tile", None, "head"),
            P("head", None),
            P(),
        ),
        out_specs=(P(None, ("head", "tile"), None), P(None, ("head", "tile"), None)),
        check_vma=False,
    )
```

```python
import functools
import math

import jax
import jax.numpy as jnp
import numpy as np
from jax import lax
from jax.experimental import pallas as pl
from jax.experimental.pallas import tpu as pltpu
from jax.sharding import PartitionSpec as P

HEADS = 12
HEAD_DIM = 128
GRID_H = 24
GRID_W = 8
PAD_ROWS = 16
EXTRA = 128
EPSILON = 1e-06
MESH = pl.DeviceIdType.MESH
F32 = jnp.float32
BF16 = jnp.bfloat16


def frequencies(pair_count):
    return np.power(10000.0, -np.arange(pair_count) / pair_count).astype(np.float32)


def layer_norm(inputs):
    average = jnp.mean(inputs, axis=-1, keepdims=True)
    centred = inputs - average
    variance = jnp.mean(centred * centred, axis=-1, keepdims=True)
    return centred * lax.rsqrt(variance + EPSILON)


def head_norm(inputs, gain_row):
    mean_square = jnp.mean(inputs * inputs, axis=-1, keepdims=True)
    return inputs * lax.rsqrt(mean_square + EPSILON) * gain_row


def matmul(a, b):
    return jnp.dot(a, b, preferred_element_type=F32)


def matmul_t(a, b):
    return lax.dot_general(a, b, (((1,), (1,)), ((), ())), preferred_element_type=F32)


def kernel(
    tiles,
    per_video,
    ext_ref,
    length_ref,
    block_mod_ref,
    head_mod_ref,
    w_qkv_ref,
    w_out_ref,
    wq_ref,
    text_k_ref,
    text_v_ref,
    wo_ref,
    head_w_ref,
    small_ref,
    hidden_out,
    velocity_out,
    rx,
    stream,
    gathered,
    q_buf,
    k_buf,
    v_buf,
    att_out,
    att_in,
    cross_in,
    part_out,
    part_in,
    own_part,
    next_rows,
    back_out,
    vel_rows,
    vel_out,
    back_in,
    vel_in,
    w_qkv,
    w_out,
    wq,
    wo,
    text_k,
    text_v,
    head_w,
    block_mod,
    head_mod,
    load_sem,
    s1_send,
    s1_recv,
    xy_send,
    xy_recv,
    back_send,
    back_recv,
):
    head = lax.axis_index("head")
    tile = lax.axis_index("tile")
    width = wq_ref.shape[0]
    group = wq_ref.shape[1]
    rows = tiles * per_video
    half_tiles = tiles // 2
    half = rows // 2
    near = tile // half_tiles
    far = 1 - near
    inner = lax.rem(tile, half_tiles)
    heads_here = group // HEAD_DIM
    factor = 1.0 / math.sqrt(HEAD_DIM)

    def partner(d):
        return lax.rem(head // 2 + d // 2, 2) * 2 + lax.rem(head % 2 + d % 2, 2)

    def tile_at(d):
        return lax.rem(tile + d + tiles, tiles)

    def tile_in(side, d):
        return side * half_tiles + lax.rem(inner + d + half_tiles, half_tiles)

    reach = [(near, d, half_tiles + d) for d in range(1, half_tiles)]
    beyond = [(far, d, d) for d in range(half_tiles)]

    loads = []

    def load(src, dst):
        copy = pltpu.make_async_copy(src, dst, load_sem.at[len(loads)])
        copy.start()
        loads.append(copy)
        return copy

    load_own = load(ext_ref.at[tile], rx.at[tile])
    load_bm = load(block_mod_ref, block_mod)
    load_hm = load(head_mod_ref.at[tile], head_mod)
    load_qkv = [
        load(
            w_qkv_ref.at[:, pl.ds(pl.multiple_of(i * width + head * group, 128), group)],
            w_qkv.at[i],
        )
        for i in range(3)
    ]

    barrier = pltpu.get_barrier_semaphore()
    for d in range(1, tiles):
        pl.semaphore_signal(barrier, inc=1, device_id=(head, tile_at(d)), device_id_type=MESH)
    for d in range(1, 4):
        pl.semaphore_signal(barrier, inc=1, device_id=(partner(d), tile), device_id_type=MESH)
    pl.semaphore_wait(barrier, tiles - 1 + 3)

    stage1 = []
    for side, d, index in reach + beyond:
        to = tile_in(side, d)
        copy = pltpu.make_async_remote_copy(
            src_ref=ext_ref.at[to],
            dst_ref=rx.at[tile],
            send_sem=s1_send.at[index],
            recv_sem=s1_recv.at[index],
            device_id=(head, to),
            device_id_type=MESH,
        )
        copy.start()
        stage1.append(copy)

    load_out = load(w_out_ref, w_out)
    load_wq = load(wq_ref, wq)
    load_tk = load(text_k_ref.at[0], text_k)
    load_tv = load(text_v_ref.at[0], text_v)
    load_wo = load(wo_ref, wo)
    load_hw = load(head_w_ref, head_w)

    def exchange(step, src, dst, d):
        return pltpu.make_async_remote_copy(
            src_ref=src,
            dst_ref=dst,
            send_sem=xy_send.at[step, d],
            recv_sem=xy_recv.at[step, d],
            device_id=(partner(d), tile),
            device_id_type=MESH,
        )

    load_own.wait()
    load_bm.wait()
    here = pl.ds(tile, 1)
    shift, scale, gate = block_mod[0, here, :], block_mod[1, here, :], block_mod[2, here, :]
    sends = []
    for part, (side, arrivals) in enumerate(((near, reach), (far, beyond))):
        for _, d, index in arrivals:
            source = tile_in(side, -d)
            pltpu.make_async_remote_copy(
                src_ref=ext_ref.at[tile],
                dst_ref=rx.at[source],
                send_sem=s1_send.at[index],
                recv_sem=s1_recv.at[index],
                device_id=(head, source),
                device_id_type=MESH,
            ).wait_recv()
        for j in range(half_tiles):
            block = rx[side * half_tiles + j].astype(F32)
            stream[side, j * per_video : j * per_video + PAD_ROWS, :] = block
        block_in = layer_norm(stream[side, :half, :width]) * (1.0 + scale) + shift
        gathered[head, side, :, :width] = block_in.astype(BF16)
        gathered[head, side, :, width:] = stream[side, :half, width:].astype(BF16)
        for d in range(1, 4):
            block = gathered.at[head, side]
            copy = exchange(part, block, block, d)
            copy.start()
            sends.append(copy)

    for copy in load_qkv:
        copy.wait()
    own_cols = pl.ds(pl.multiple_of(head * group, 128), group)
    q_gain = small_ref[0:1, own_cols]
    k_gain = small_ref[1:2, own_cols]
    lane = lax.broadcasted_iota(jnp.int32, (1, HEAD_DIM), 1)
    sign = jnp.where(lane < HEAD_DIM // 2, -1.0, 1.0)
    for d in range(4):
        slot = partner(d)
        if d > 0:
            for part, side in enumerate((near, far)):
                block = gathered.at[slot, side]
                exchange(part, block, block, d).wait_recv()
        tokens = gathered[slot, :, :, :width].reshape(rows, width)
        places = gathered[slot, :, :, width:].reshape(rows, EXTRA)
        angles = places.astype(F32) * small_ref[4:5, :EXTRA]
        cosine = jnp.cos(angles)
        sine = jnp.sin(angles) * sign
        for i, (gain, buf) in enumerate(((q_gain, q_buf), (k_gain, k_buf))):
            raw = matmul(tokens, w_qkv[i])
            for g in range(heads_here):
                cols = slice(g * HEAD_DIM, (g + 1) * HEAD_DIM)
                u = head_norm(raw[:, cols], gain[:, cols])
                turned = u * cosine + pltpu.roll(u, HEAD_DIM // 2, 1) * sine
                buf[slot, :, cols] = turned.astype(BF16)
        v_buf[slot] = matmul(tokens, w_qkv[2]).astype(BF16)

    for d in (1, 2, 3, 0):
        slot = partner(d)
        for g in range(heads_here):
            cols = slice(g * HEAD_DIM, (g + 1) * HEAD_DIM)
            keys = k_buf[:, :, cols].reshape(4 * rows, HEAD_DIM)
            values = v_buf[:, :, cols].reshape(4 * rows, HEAD_DIM)
            weights = jnp.exp(matmul_t(q_buf[slot, :, cols], keys) * factor)
            total = jnp.sum(weights, axis=-1, keepdims=True)
            mixed = matmul(weights.astype(BF16), values) / total
            att_out[slot, :, cols] = mixed.astype(BF16)
        if d > 0:
            copy = exchange(2, att_out.at[slot], att_in.at[head], d)
            copy.start()
            sends.append(copy)

    load_out.wait()
    update = matmul(att_out[head], w_out[pl.ds(pl.multiple_of(head * group, 128), group), :])
    for d in range(1, 4):
        slot = partner(d)
        exchange(2, att_out.at[slot], att_in.at[slot], d).wait_recv()
        update += matmul(att_in[slot], w_out[pl.ds(pl.multiple_of(slot * group, 128), group), :])
    for side in range(2):
        after_self = stream[side, :half, :width] + gate * update[side * half : (side + 1) * half]
        stream[side, :half, :width] = after_self
        cross_in[head, side] = (layer_norm(after_self) * small_ref[2:3, :]).astype(BF16)
    for part, side in enumerate((far, near)):
        for d in range(1, 4):
            block = cross_in.at[head, side]
            copy = exchange(3 + part, block, block, d)
            copy.start()
            sends.append(copy)

    for copy in (load_wq, load_tk, load_tv, load_wo):
        copy.wait()
    position = lax.broadcasted_iota(jnp.int32, (1, text_k.shape[0]), 1)
    live = jnp.where(position < length_ref[0], 1.0, 0.0)
    for part, side in enumerate((far, near)):
        for d in range(4):
            slot = partner(d)
            if d > 0:
                block = cross_in.at[slot, side]
                exchange(3 + part, block, block, d).wait_recv()
            raw = matmul(cross_in[slot, side], wq[...])
            mixes = []
            for g in range(heads_here):
                cols = slice(g * HEAD_DIM, (g + 1) * HEAD_DIM)
                query = head_norm(raw[:, cols], small_ref[3:4, cols]).astype(BF16)
                weights = jnp.exp(matmul_t(query, text_k[:, cols]) * factor) * live
                total = jnp.sum(weights, axis=-1, keepdims=True)
                mixes.append((matmul(weights.astype(BF16), text_v[:, cols]) / total).astype(BF16))
            product = matmul(jnp.concatenate(mixes, axis=-1), wo[...])
            if d == 0:
                own_part[part] = product
            else:
                part_out[part, d - 1] = product.astype(BF16)
                copy = exchange(5 + part, part_out.at[part, d - 1], part_in.at[part, d - 1], d)
                copy.start()
                sends.append(copy)

    def giving(kind, src, dst, to, index):
        return pltpu.make_async_remote_copy(
            src_ref=src,
            dst_ref=dst,
            send_sem=back_send.at[kind, index],
            recv_sem=back_recv.at[kind, index],
            device_id=(head, to),
            device_id_type=MESH,
        )

    load_hm.wait()
    load_hw.wait()
    next_rows[half:, :] = jnp.zeros((PAD_ROWS, width), F32)
    vel_rows[...] = jnp.zeros_like(vel_rows)
    for part, (side, leaving) in enumerate(((far, beyond), (near, reach))):
        total = own_part[part]
        for d in range(1, 4):
            exchange(
                5 + part, part_out.at[part, d - 1], part_in.at[part, d - 1], d
            ).wait_recv()
            total += part_in[part, d - 1].astype(F32)
        after_cross = stream[side, :half, :width] + total.astype(BF16).astype(F32)
        next_rows[:half, :] = after_cross
        for j in range(half_tiles):
            block = next_rows[j * per_video : j * per_video + PAD_ROWS, :]
            back_out[side * half_tiles + j] = block.astype(BF16)
        for _, d, index in leaving:
            to = tile_in(side, d)
            copy = giving(0, back_out.at[to], back_in.at[tile], to, index)
            copy.start()
            sends.append(copy)
        head_in = layer_norm(after_cross) * (1.0 + head_mod[1:2, :]) + head_mod[0:1, :]
        vel_rows[:half, : head_w.shape[0]] = matmul_t(head_in.astype(BF16), head_w[...])
        for j in range(half_tiles):
            vel_out[side * half_tiles + j] = vel_rows[j * per_video : j * per_video + PAD_ROWS, :]
        for _, d, index in leaving:
            to = tile_in(side, d)
            copy = giving(1, vel_out.at[to], vel_in.at[tile], to, index)
            copy.start()
            sends.append(copy)
    hidden_out[tile] = back_out[tile]
    velocity_out[tile] = vel_out[tile]
    for side, d, index in reach + beyond:
        source = tile_in(side, -d)
        giving(0, back_out.at[source], back_in.at[source], source, index).wait_recv()
        hidden_out[source] = back_in[source]
        giving(1, vel_out.at[source], vel_in.at[source], source, index).wait_recv()
        velocity_out[source] = vel_in[source]
    for copy in stage1 + sends:
        copy.wait_send()


def local(
    hidden,
    latent,
    cell_map,
    text_lengths,
    block_modulation,
    head_modulation,
    step_sizes,
    w_qkv,
    self_q_gain,
    self_k_gain,
    w_out,
    cross_gain,
    cross_wq,
    cross_q_gain,
    text_keys,
    text_values,
    cross_wo,
    head_w,
):
    head_count = lax.axis_size("head")
    tiles = lax.axis_size("tile")
    videos, per_video, width = hidden.shape
    group = width // head_count
    rows = tiles * per_video
    text = text_keys.shape[1]
    channels = head_w.shape[1]
    sixth = HEAD_DIM // 6
    time_pairs = HEAD_DIM // 2 - 2 * sixth

    lane = jnp.arange(EXTRA) % (HEAD_DIM // 2)
    cells = cell_map[..., None]
    places = jnp.where(
        lane < time_pairs,
        cells // (GRID_H * GRID_W),
        jnp.where(lane < time_pairs + sixth, cells // GRID_W % GRID_H, cells % GRID_W),
    ).astype(BF16)
    half = np.concatenate([frequencies(n) for n in (time_pairs, sixth, sixth)])
    freq = np.zeros((width,), np.float32)
    freq[:EXTRA] = np.concatenate([half, half])
    small = jnp.stack(
        [self_q_gain, self_k_gain, cross_gain, jnp.pad(cross_q_gain, (0, width - group)), freq]
    )
    ext = jnp.pad(
        jnp.concatenate([hidden, places], axis=-1),
        ((0, 0), (0, PAD_ROWS - per_video), (0, 0)),
    )
    any_spec = pl.BlockSpec(memory_space=pl.ANY)
    vmem = pl.BlockSpec(memory_space=pltpu.VMEM)
    smem = pl.BlockSpec(memory_space=pltpu.SMEM)
    dma = pltpu.SemaphoreType.DMA
    hidden_pad, velocity = pl.pallas_call(
        functools.partial(kernel, tiles, per_video),
        out_shape=(
            jax.ShapeDtypeStruct((tiles, PAD_ROWS, width), BF16),
            jax.ShapeDtypeStruct((tiles, PAD_ROWS, 128), F32),
        ),
        in_specs=[any_spec, smem] + [any_spec] * 9 + [vmem],
        out_specs=(vmem, vmem),
        scratch_shapes=[
            pltpu.VMEM((tiles, PAD_ROWS, width + EXTRA), BF16),
            pltpu.VMEM((2, rows // 2 + PAD_ROWS, width + EXTRA), F32),
            pltpu.VMEM((head_count, 2, rows // 2, width + EXTRA), BF16),
            pltpu.VMEM((head_count, rows, group), BF16),
            pltpu.VMEM((head_count, rows, group), BF16),
            pltpu.VMEM((head_count, rows, group), BF16),
            pltpu.VMEM((head_count, rows, group), BF16),
            pltpu.VMEM((head_count, rows, group), BF16),
            pltpu.VMEM((head_count, 2, rows // 2, width), BF16),
            pltpu.VMEM((2, 3, rows // 2, width), BF16),
            pltpu.VMEM((2, 3, rows // 2, width), BF16),
            pltpu.VMEM((2, rows // 2, width), F32),
            pltpu.VMEM((rows // 2 + PAD_ROWS, width), F32),
            pltpu.VMEM((tiles, PAD_ROWS, width), BF16),
            pltpu.VMEM((rows // 2 + PAD_ROWS, 128), F32),
            pltpu.VMEM((tiles, PAD_ROWS, 128), F32),
            pltpu.VMEM((tiles, PAD_ROWS, width), BF16),
            pltpu.VMEM((tiles, PAD_ROWS, 128), F32),
            pltpu.VMEM((3, width, group), BF16),
            pltpu.VMEM((width, width), BF16),
            pltpu.VMEM((width, group), BF16),
            pltpu.VMEM((group, width), BF16),
            pltpu.VMEM((text, group), BF16),
            pltpu.VMEM((text, group), BF16),
            pltpu.VMEM((channels, width), BF16),
            pltpu.VMEM((3, videos, width), F32),
            pltpu.VMEM((2, width), F32),
            dma((12,)),
            dma((tiles,)),
            dma((tiles,)),
            dma((7, 4)),
            dma((7, 4)),
            dma((2, tiles)),
            dma((2, tiles)),
        ],
        compiler_params=pltpu.CompilerParams(
            collective_id=0, has_side_effects=True, vmem_limit_bytes=60 * 1024 * 1024
        ),
    )(
        ext,
        text_lengths,
        block_modulation.transpose(1, 0, 2),
        head_modulation,
        w_qkv,
        w_out,
        cross_wq,
        text_keys,
        text_values,
        cross_wo,
        head_w.T,
        small,
    )
    hidden_next = hidden_pad[:, :per_video]
    latent_next = latent + step_sizes[:, None, None] * velocity[:, :per_video, :channels]
    return (hidden_next, latent_next)


def solution(mesh):
    return jax.shard_map(
        local,
        mesh=mesh,
        in_specs=(
            P(None, ("head", "tile"), None),
            P(None, ("head", "tile"), None),
            P(None, ("head", "tile")),
            P("tile"),
            P(),
            P(),
            P(),
            P(),
            P(),
            P(),
            P(),
            P(),
            P(None, "head"),
            P("head"),
            P("tile", None, "head"),
            P("tile", None, "head"),
            P("head", None),
            P(),
        ),
        out_specs=(P(None, ("head", "tile"), None), P(None, ("head", "tile"), None)),
        check_vma=False,
    )
```
